32 devices in a mesh: member: 8 (over z, core), expert: 4 (over y, x).
Axes of the slice: x: 2, y: 2, z: 4, core: 2. Of those that a mesh axis runs over, the one named last changes fastest.
Arguments:
- tokens: bfloat16 [4096, 2048], P(('member', 'expert')), may hold values from -6 to 6
- cotangent: bfloat16 [4096, 2048], P(('member', 'expert')), may hold values from -6 to 6
- routes: int32 [4096, 2], P(('member', 'expert')), may hold values from 0 to 3, all different within a row; in each aligned block of 128 rows (0 to 127, 128 to 255, ...) at most 128 rows name the same one
- gate_probs: bfloat16 [4096, 2], P(('member', 'expert')), may hold values from 0.099609375 to 0.8984375
- weight_in: bfloat16 [8192, 512], P('member', 'expert'), may hold values from -6 to 6
- weight_out: bfloat16 [8192, 512], P('member', 'expert'), may hold values from -6 to 6
- moment_in: float32 [8192, 512], P('member', 'expert'), may hold values from -0.4 to 0.4
- square_in: float32 [8192, 512], P('member', 'expert'), may hold values from 0.0025 to 0.25
- moment_out: float32 [8192, 512], P('member', 'expert'), may hold values from -0.4 to 0.4
- square_out: float32 [8192, 512], P('member', 'expert'), may hold values from 0.0025 to 0.25
- parents: int32 [4], replicated, may hold values from 0 to 3, as said below
- own_rates: float32 [4], replicated, may hold values from 0.05 to 0.5
- perturbed: float32 [4], replicated, may hold values from 0.05 to 0.5
Outputs:
- new_in: bfloat16 [8192, 512], P('member', 'expert')
- new_out: bfloat16 [8192, 512], P('member', 'expert')
- layer_out: bfloat16 [4096, 2048], P(('member', 'expert'))
The draws below stay inside these ranges and needn't reach their ends.
Inputs may be any that keep to these rules, and one draw needn't show every extreme that they name: parents[m] = m for all members but one to at most 2; those have distinct parents, each of which is its own parent. `routes`: each row names two different experts. In the rows of one device no expert is named by more than 128 rows, and in every draw some expert is named by exactly 128 rows of some device.
All inputs are finite; a program needn't handle non-finite values.
Results may differ from the reference program's by a relative error of at most 0.0058.
Values may be sent and summed in bfloat16 or wider, within the bound.
A program may use at most 64 MiB of HBM per device.

```python
import math
import jax
import jax.numpy as jnp
import numpy as np
from jax import lax

D = 2048
HID = 128
TOK_DEV = 128
EXPERTS = 4
MEMBERS = 4
CAP = 128
TOKENS = 4096


def draw_parents(key, part):
    first_key = jax.random.fold_in(key, 11)
    second_key = jax.random.fold_in(key, 12)
    half_count = MEMBERS // 2
    shuffled = jax.random.permutation(first_key, MEMBERS).astype(jnp.int32)
    identity = jnp.arange(MEMBERS, dtype=jnp.int32)
    losing = shuffled[:half_count]
    winning = shuffled[half_count:]
    copying = jax.random.randint(second_key, (), 1, half_count + 1).astype(jnp.int32)
    slot_ids = jnp.arange(half_count, dtype=jnp.int32)
    chosen = jnp.where(slot_ids < copying, winning, losing)
    return identity.at[losing].set(chosen)


def block_levels(key, extent, pieces, smallest, largest):
    level = 1.0
    for dim, blocks in pieces:
        draws = jax.random.uniform(jax.random.fold_in(jax.random.fold_in(key, 6), dim), (blocks,), jnp.float32, smallest / len(pieces), largest / len(pieces))
        level = level * jnp.repeat(jnp.exp(draws), extent[dim] // blocks).reshape((-1,) + (1,) * (len(extent) - 1 - dim))
    return level


def deal_out(key, own, number, rows, number_of, top, bound, slope):
    sequence = jax.random.permutation(key, number_of)
    packed, common = portions_of(number_of, rows * top, bound, slope, True), portions_of(number_of, rows * top, bound, slope, False)
    places = jnp.arange(number_of)

    def named(lengths, offset_by):
        used = int((lengths > 0).sum())
        fixed = max(1, used // 4)
        passed = fixed + (places - fixed + offset_by * (used - fixed)) % max(1, number_of - fixed)
        return jnp.zeros((number_of,), jnp.int32).at[sequence[jnp.where(places < fixed, places, passed)]].set(jnp.asarray(lengths, jnp.int32))

    lengths = jnp.where(number % 4 == 0, named(packed, number // 4), named(common, number - number // 4 - 1))
    mixed = jax.random.permutation(jax.random.fold_in(own, 3), number_of)
    donor, taker = mixed[0:number_of // 2 * 2:2], mixed[1:number_of // 2 * 2:2]
    room = jnp.minimum(lengths[donor] - 1, bound - lengths[taker]) // 2
    room = jnp.where((donor == sequence[0]) | (taker == sequence[0]) | (lengths[taker] == 0), 0, jnp.maximum(room, 0))
    passed = jax.random.randint(jax.random.fold_in(own, 4), (number_of // 2,), 0, 1 << 20) % (room + 1)
    lengths = lengths.at[donor].add(-passed).at[taker].add(passed)
    members = jnp.searchsorted(jnp.cumsum(lengths), jnp.arange(rows * top), side="right").astype(jnp.int32)
    listing = members.reshape(top, rows).T
    listing = listing[jax.random.permutation(jax.random.fold_in(own, 1), rows)]
    offset_by = jax.random.randint(jax.random.fold_in(own, 2), (rows, 1), 0, top)
    return jnp.take_along_axis(listing, (jnp.arange(top)[None, :] + offset_by) % top, axis=1)


def portions_of(amount, total, limit, skew, full):
    weights = [(1 << 20) // math.isqrt(rank ** skew) + 1 for rank in range(1, amount + 1)]
    largest = limit if full else min(limit, max(-(-total // amount), total * weights[0] // sum(weights)))
    least = 1 if total - largest >= amount - 1 else 0
    counts, rest = [largest] + [least] * (amount - 1), total - largest - least * (amount - 1)
    while rest > 0:
        movable = [i for i in range(1, amount) if counts[i] < largest] or [i for i in range(1, amount) if counts[i] < limit]
        pool, budget = sum([weights[i] for i in movable]), rest
        for i in movable:
            addition = min(limit - counts[i], max(1, budget * weights[i] // pool), rest)
            counts[i] = counts[i] + addition
            rest = rest - addition
    return np.array(counts)


def gaussian(rng, extent, scale, bound, cuts=(), kind=jnp.bfloat16):
    drawn = jax.random.normal(rng, extent, jnp.float32) * scale
    if len(cuts) > 0:
        drawn = block_levels(rng, extent, cuts, -0.22, 0.18) * drawn
    return jnp.clip(drawn, min=-bound, max=bound).astype(kind)


def setup_inputs(seed: int = 0) -> dict:
    keys = jax.random.split(jax.random.key(seed), 14)
    tokens = gaussian(keys[0], (TOKENS, D), 1.0, 6.0, ((0, 32),))
    cotangent = gaussian(keys[1], (TOKENS, D), 1.0, 6.0, ((0, 32),))
    routes_keys = jax.random.split(jax.random.fold_in(keys[2], 1), TOKENS // TOK_DEV)
    routes_turns = jax.random.permutation(jax.random.fold_in(keys[2], 3), TOKENS // TOK_DEV)
    routes = jax.vmap(lambda own, number: deal_out(jax.random.fold_in(keys[2], 2), own, number, TOK_DEV, EXPERTS, 2, CAP, 2))(routes_keys, routes_turns).reshape((TOKENS, 2))
    gate_probs = jnp.clip(0.099609375 + 0.7988281 * jax.random.uniform(keys[3], (TOKENS, 2), jnp.float32) ** block_levels(keys[3], (TOKENS, 2), ((0, 32),), -0.2, 0.2), 0.099609375, 0.8984375).astype(jnp.bfloat16)
    weight_in = gaussian(keys[4], (MEMBERS * D, EXPERTS * HID), 1.0, 6.0, ((0, 8), (1, 4)))
    weight_out = gaussian(keys[5], (MEMBERS * D, EXPERTS * HID), 1.0, 6.0, ((0, 8), (1, 4)))
    moment_in = gaussian(keys[6], (MEMBERS * D, EXPERTS * HID), 0.05, 0.4, ((0, 8), (1, 4)), jnp.float32)
    square_in = jnp.clip(jnp.exp(math.log(0.25) - 4.6051702 * jax.random.uniform(keys[7], (MEMBERS * D, EXPERTS * HID), jnp.float32) ** block_levels(keys[7], (MEMBERS * D, EXPERTS * HID), ((0, 8), (1, 4)), -0.2, 0.2)), 0.0025, 0.25)
    moment_out = gaussian(keys[8], (MEMBERS * D, EXPERTS * HID), 0.05, 0.4, ((0, 8), (1, 4)), jnp.float32)
    square_out = jnp.clip(jnp.exp(math.log(0.25) - 4.6051702 * jax.random.uniform(keys[9], (MEMBERS * D, EXPERTS * HID), jnp.float32) ** block_levels(keys[9], (MEMBERS * D, EXPERTS * HID), ((0, 8), (1, 4)), -0.2, 0.2)), 0.0025, 0.25)
    parents = draw_parents(jax.random.fold_in(keys[13], 71), 0)
    own_rates = jnp.clip(jnp.exp(jax.random.uniform(keys[11], (MEMBERS,), jnp.float32, math.log(0.05), math.log(0.5))), 0.05, 0.5)
    perturbed = jnp.clip(jnp.exp(jax.random.uniform(keys[12], (MEMBERS,), jnp.float32, math.log(0.05), math.log(0.5))), 0.05, 0.5)
    return dict(tokens=tokens, cotangent=cotangent, routes=routes, gate_probs=gate_probs, weight_in=weight_in, weight_out=weight_out, moment_in=moment_in, square_in=square_in, moment_out=moment_out, square_out=square_out, parents=parents, own_rates=own_rates, perturbed=perturbed)


beta_first = 0.9
beta_second = 0.999
adam_floor = 1e-08

def gelu_back(pre_act, upstream):
    _, pullback = jax.vjp(lambda inner: jax.nn.gelu(inner, approximate=True), pre_act)
    return pullback(upstream)[0]

def adam_step(param, moment, square, gradient, step_rate):
    moment_new = beta_first * moment + (1.0 - beta_first) * gradient
    square_new = beta_second * square + (1.0 - beta_second) * gradient * gradient
    moved = param.astype(jnp.float32) - step_rate * moment_new / (jnp.sqrt(square_new) + adam_floor)
    return moved.astype(jnp.bfloat16)

def member_step(member, tokens, cotangent, routes, gate_probs, weight_in, weight_out, moment_in, square_in, moment_out, square_out, parents, own_rates, perturbed):
    tok_member = TOK_DEV * 2 * EXPERTS
    parent = jnp.take(parents, member)
    step_rate = jnp.where(parent != member, jnp.take(perturbed, member), jnp.take(own_rates, member))
    row_start = (parent * D).astype(jnp.int32)
    start_in = lax.dynamic_slice_in_dim(weight_in, row_start, D, 0)
    start_out = lax.dynamic_slice_in_dim(weight_out, row_start, D, 0)
    tok_start = (member * tok_member).astype(jnp.int32)
    inputs = lax.dynamic_slice_in_dim(tokens, tok_start, tok_member, 0)
    cotan = lax.dynamic_slice_in_dim(cotangent, tok_start, tok_member, 0)
    member_routes = lax.dynamic_slice_in_dim(routes, tok_start, tok_member, 0)
    member_gates = lax.dynamic_slice_in_dim(gate_probs, tok_start, tok_member, 0).astype(jnp.float32)
    expert_ids = jnp.arange(EXPERTS, dtype=jnp.int32)
    gate_table = lax.optimization_barrier(jnp.sum(jnp.where(member_routes[:, :, None] == expert_ids[None, None, :], member_gates[:, :, None], 0.0), axis=1))
    gate_cols = jnp.repeat(gate_table, HID, axis=1)
    pre_act = jnp.dot(inputs, start_in, preferred_element_type=jnp.float32) * D ** (-0.5)
    hidden = jax.nn.gelu(pre_act, approximate=True).astype(jnp.bfloat16)
    layer_sum = jnp.zeros((tok_member, D), jnp.float32)
    for expert in range(EXPERTS):
        columns = slice(expert * HID, (expert + 1) * HID)
        expert_out = lax.dot_general(hidden[:, columns], start_out[:, columns], (((1,), (1,)), ((), ())), preferred_element_type=jnp.float32) * HID ** (-0.5)
        rounded = lax.optimization_barrier(expert_out.astype(jnp.bfloat16)).astype(jnp.float32)
        layer_sum = layer_sum + gate_table[:, expert:expert + 1] * rounded
    gated_hidden = (gate_cols * hidden.astype(jnp.float32)).astype(jnp.bfloat16)
    grad_out = lax.dot_general(cotan, gated_hidden, (((0,), (0,)), ((), ())), preferred_element_type=jnp.float32) * HID ** (-0.5)
    back_hidden = jnp.dot(cotan, start_out, preferred_element_type=jnp.float32) * HID ** (-0.5) * gate_cols
    back_pre = gelu_back(pre_act, back_hidden).astype(jnp.bfloat16)
    grad_in = lax.dot_general(inputs, back_pre, (((0,), (0,)), ((), ())), preferred_element_type=jnp.float32) * D ** (-0.5)
    new_in = adam_step(start_in, lax.dynamic_slice_in_dim(moment_in, row_start, D, 0), lax.dynamic_slice_in_dim(square_in, row_start, D, 0), grad_in, step_rate)
    new_out = adam_step(start_out, lax.dynamic_slice_in_dim(moment_out, row_start, D, 0), lax.dynamic_slice_in_dim(square_out, row_start, D, 0), grad_out, step_rate)
    return (new_in, new_out, layer_sum.astype(jnp.bfloat16))

def reference(tokens, cotangent, routes, gate_probs, weight_in, weight_out, moment_in, square_in, moment_out, square_out, parents, own_rates, perturbed):

    def per_member(member):
        return member_step(member, tokens, cotangent, routes, gate_probs, weight_in, weight_out, moment_in, square_in, moment_out, square_out, parents, own_rates, perturbed)
    new_in, new_out, layer_out = lax.map(per_member, jnp.arange(MEMBERS, dtype=jnp.int32))
    return (new_in.reshape(MEMBERS * D, EXPERTS * HID), new_out.reshape(MEMBERS * D, EXPERTS * HID), layer_out.reshape(TOKENS, D))
```

```python
import functools

import jax
import jax.numpy as jnp
from jax import lax
from jax.experimental import pallas as pl
from jax.experimental.pallas import tpu as pltpu
from jax.sharding import PartitionSpec as P

beta_first = 0.9
beta_second = 0.999
adam_floor = 1e-08


def for_sending(shard):

    def short(part):
        return part.astype(jnp.bfloat16) if part.dtype == jnp.float32 else part

    return jax.tree.map(short, shard)


def partner(shard, axis, bit):
    return lax.ppermute(shard, axis, [(i, i ^ 1 << bit) for i in range(lax.axis_size(axis))])


def gelu_back(pre_act, upstream):
    _, pullback = jax.vjp(lambda inner: jax.nn.gelu(inner, approximate=True), pre_act)
    return pullback(upstream)[0]


def adam_step(param, moment, square, gradient, step_rate):
    moment_new = beta_first * moment + (1.0 - beta_first) * gradient
    square_new = beta_second * square + (1.0 - beta_second) * gradient * gradient
    moved = param.astype(jnp.float32) - step_rate * moment_new / (jnp.sqrt(square_new) + adam_floor)
    return moved.astype(jnp.bfloat16)


def pick_rows(pieces, choose):
    return tuple((jnp.take(piece, choose, axis=0) for piece in pieces))


def relay_together(arrays, choose, devices):
    flat = [array.reshape(devices, -1) for array in arrays]
    sent = (
        lax.all_to_all(
            flat[0].astype(jnp.bfloat16), "member", split_axis=0, concat_axis=0, tiled=True
        ).astype(jnp.float32),
        lax.all_to_all(
            flat[1].astype(jnp.bfloat16), "member", split_axis=0, concat_axis=0, tiled=True
        ).astype(jnp.float32),
        lax.all_to_all(
            flat[2].astype(jnp.bfloat16), "member", split_axis=0, concat_axis=0, tiled=True
        ).astype(jnp.float32),
        lax.all_to_all(
            flat[3].astype(jnp.bfloat16), "member", split_axis=0, concat_axis=0, tiled=True
        ).astype(jnp.float32),
        lax.all_to_all(
            flat[4].astype(jnp.bfloat16), "member", split_axis=0, concat_axis=0, tiled=True
        ).astype(jnp.float32),
        lax.all_to_all(
            flat[5].astype(jnp.bfloat16), "member", split_axis=0, concat_axis=0, tiled=True
        ).astype(jnp.float32),
    )
    picked = pick_rows(sent, choose)
    landed = (
        lax.all_to_all(for_sending(picked[0]), "member", split_axis=0, concat_axis=0, tiled=True),
        lax.all_to_all(for_sending(picked[1]), "member", split_axis=0, concat_axis=0, tiled=True),
        lax.all_to_all(for_sending(picked[2]), "member", split_axis=0, concat_axis=0, tiled=True),
        lax.all_to_all(for_sending(picked[3]), "member", split_axis=0, concat_axis=0, tiled=True),
        lax.all_to_all(for_sending(picked[4]), "member", split_axis=0, concat_axis=0, tiled=True),
        lax.all_to_all(for_sending(picked[5]), "member", split_axis=0, concat_axis=0, tiled=True),
    )
    return [piece.reshape(array.shape) for piece, array in zip(landed, arrays)]


def train_pass(start_in, start_out, tokens, cotangent, routes, gate_probs, upper_half):
    half_rows = start_in.shape[0]
    width = tokens.shape[1]
    scale_model = width ** (-0.5)
    scale_hidden = start_in.shape[1] ** (-0.5)
    partner_in, partner_out = partner((start_in, start_out), "member", 0)
    is_upper = upper_half == 1
    full_in = jnp.where(
        is_upper,
        jnp.concatenate([partner_in, start_in], 0),
        jnp.concatenate([start_in, partner_in], 0),
    )
    full_out = jnp.where(
        is_upper,
        jnp.concatenate([partner_out, start_out], 0),
        jnp.concatenate([start_out, partner_out], 0),
    )
    experts = lax.axis_size("expert")
    tok_rows = tokens.shape[0]
    capacity = min(tok_rows, 5 * tok_rows // experts)
    flat_route = routes.reshape(-1)
    expert_ids = jnp.arange(experts, dtype=jnp.int32)
    onehot = (flat_route[:, None] == expert_ids[None, :]).astype(jnp.int32)
    places = jnp.arange(flat_route.shape[0], dtype=jnp.int32)
    before = (places[None, :] < places[:, None]).astype(jnp.float32)
    earlier = jnp.dot(before, onehot.astype(jnp.float32)).astype(jnp.int32)
    position_in = jnp.sum(earlier * onehot, axis=1)
    slot_of = flat_route * capacity + position_in
    slot_ids = jnp.arange(experts * capacity, dtype=jnp.int32)
    pairing = slot_of[None, :] == slot_ids[:, None]
    filled = jnp.any(pairing, axis=1)
    assign_ids = jnp.arange(flat_route.shape[0], dtype=jnp.int32)
    assigned = jnp.sum(jnp.where(pairing, assign_ids[None, :], 0), axis=1)
    token_of = jnp.where(filled, assigned // 2, tok_rows)
    zero_row = jnp.zeros((1, width), jnp.bfloat16)
    send_tokens = jnp.take(jnp.concatenate([tokens, zero_row], 0), token_of, axis=0).reshape(
        experts, capacity, width
    )
    send_cotan = jnp.take(jnp.concatenate([cotangent, zero_row], 0), token_of, axis=0).reshape(
        experts, capacity, width
    )
    send_gates = jnp.where(
        filled, jnp.take(gate_probs.reshape(-1), assigned), jnp.zeros((), jnp.bfloat16)
    ).reshape(experts, capacity)
    got_tokens, got_cotan, got_gates = (
        lax.all_to_all(send_tokens, "expert", split_axis=0, concat_axis=0, tiled=True),
        lax.all_to_all(send_cotan, "expert", split_axis=0, concat_axis=0, tiled=True),
        lax.all_to_all(send_gates, "expert", split_axis=0, concat_axis=0, tiled=True),
    )
    rows_tokens = got_tokens.reshape(-1, width)
    rows_cotan = got_cotan.reshape(-1, width)
    rows_gates = got_gates.reshape(-1, 1).astype(jnp.float32)
    pre_act = jnp.dot(rows_tokens, full_in, preferred_element_type=jnp.float32) * scale_model
    hidden = jax.nn.gelu(pre_act, approximate=True).astype(jnp.bfloat16)
    expert_out = (
        lax.dot_general(
            hidden, full_out, (((1,), (1,)), ((), ())), preferred_element_type=jnp.float32
        )
        * scale_hidden
    ).astype(jnp.bfloat16)
    returned = lax.all_to_all(
        expert_out.reshape(experts, capacity, width),
        "expert",
        split_axis=0,
        concat_axis=0,
        tiled=True,
    )
    gathered = jnp.take(returned.reshape(-1, width), slot_of, axis=0).reshape(tok_rows, 2, width)
    weighted = gathered.astype(jnp.float32) * gate_probs.astype(jnp.float32)[:, :, None]
    layer_out = (weighted[:, 0] + weighted[:, 1]).astype(jnp.bfloat16)
    gated_hidden = (rows_gates * hidden.astype(jnp.float32)).astype(jnp.bfloat16)
    grad_out_full = (
        lax.dot_general(
            rows_cotan, gated_hidden, (((0,), (0,)), ((), ())), preferred_element_type=jnp.float32
        )
        * scale_hidden
    )
    back_hidden = (
        jnp.dot(rows_cotan, full_out, preferred_element_type=jnp.float32)
        * scale_hidden
        * rows_gates
    )
    back_pre = gelu_back(pre_act, back_hidden).astype(jnp.bfloat16)
    grad_in_full = (
        lax.dot_general(
            rows_tokens, back_pre, (((0,), (0,)), ((), ())), preferred_element_type=jnp.float32
        )
        * scale_model
    )
    other_start = (1 - upper_half) * half_rows
    own_start = upper_half * half_rows
    give_in = lax.dynamic_slice_in_dim(grad_in_full, other_start, half_rows, 0)
    give_out = lax.dynamic_slice_in_dim(grad_out_full, other_start, half_rows, 0)
    taken_in, taken_out = (
        partner(give_in.astype(jnp.bfloat16), "member", 0).astype(give_in.dtype),
        partner(give_out.astype(jnp.bfloat16), "member", 0).astype(give_out.dtype),
    )
    grad_in = lax.dynamic_slice_in_dim(grad_in_full, own_start, half_rows, 0) + taken_in
    grad_out = lax.dynamic_slice_in_dim(grad_out_full, own_start, half_rows, 0) + taken_out
    return (grad_in, grad_out, layer_out)


def on_device(
    tokens,
    cotangent,
    routes,
    gate_probs,
    weight_in,
    weight_out,
    moment_in,
    square_in,
    moment_out,
    square_out,
    parents,
    own_rates,
    perturbed,
):
    devices = lax.axis_size("member")
    position = lax.axis_index("member")
    member = position // 2
    upper_half = position % 2
    member_ids = jnp.arange(parents.shape[0], dtype=jnp.int32)
    device_ids = jnp.arange(devices, dtype=jnp.int32)
    from_device = 2 * jnp.take(parents, device_ids // 2) + device_ids % 2
    chosen_rates = jnp.where(parents != member_ids, perturbed, own_rates)
    own_rate = jnp.take(chosen_rates, member)
    landed = relay_together(
        (
            weight_in.astype(jnp.float32),
            weight_out.astype(jnp.float32),
            moment_in,
            square_in,
            moment_out,
            square_out,
        ),
        from_device,
        devices,
    )
    start_in = landed[0].astype(jnp.bfloat16)
    start_out = landed[1].astype(jnp.bfloat16)
    grad_in, grad_out, layer_out = train_pass(
        start_in, start_out, tokens, cotangent, routes, gate_probs, upper_half
    )
    new_in = adam_step(start_in, landed[2], landed[3], grad_in, own_rate)
    new_out = adam_step(start_out, landed[4], landed[5], grad_out, own_rate)
    return (new_in, new_out, layer_out)


MESH = pl.DeviceIdType.MESH
PARTS = 2
GELU_C = 0.7978845608028654
GELU_A = 0.044715


def gelu_tanh(x):
    return jnp.tanh(GELU_C * (x + GELU_A * x * x * x))


def fused_kernel(rounds, members, *refs):
    (flags, rate_ref, tok, cot, gates, w_in, w_out, m_in, s_in, m_out, s_out,
     new_in, new_out, layer_out,
     own, in_z, out_z, tok_all, cot_all, gate_all, full_in, full_out,
     pre_s, hid_s, gated_s, back_s, own_part, keep_a, keep_b, send_a, send_b, got_a, got_b,
     send2, got2, grad_own, grad_send, grad_got,
     z_send, z_recv, p_send, p_recv, g_send, g_recv, w_send, w_recv, r_send, r_recv, d_send, d_recv, l_sem,
     ) = refs
    position = lax.axis_index("member")
    expert = lax.axis_index("expert")
    m = position // 2
    c = position % 2
    ex, ey = expert % 2, expert // 2
    rows, width = tok.shape
    half = width // 2
    rhalf = rows // 2
    wrows, hid = w_in.shape
    crow = wrows // PARTS
    n_chunk = 6 * PARTS
    scale_model = width ** (-0.5)
    scale_hidden = hid ** (-0.5)

    def peer(t):
        return {"expert": ((ey + t // 2) % 2) * 2 + (ex + t % 2) % 2}

    core_peer = {"member": m * 2 + (1 - c)}
    up = {"member": lax.rem(m + 1, members) * 2 + c}
    down = {"member": lax.rem(m + members - 1, members) * 2 + c}
    has_up = m < members - 1
    has_down = m > 0

    barrier = pltpu.get_barrier_semaphore()
    for t in (1, 2, 3):
        pl.semaphore_signal(barrier, inc=1, device_id=peer(t), device_id_type=MESH)
    pl.semaphore_signal(barrier, inc=1, device_id=core_peer, device_id_type=MESH)

    @pl.when(has_up)
    def _():
        pl.semaphore_signal(barrier, inc=1, device_id=up, device_id_type=MESH)

    @pl.when(has_down)
    def _():
        pl.semaphore_signal(barrier, inc=1, device_id=down, device_id_type=MESH)

    def cast(source, index):
        for part in range(PARTS):
            own[index * PARTS + part] = source[pl.ds(part * crow, crow), :].astype(jnp.bfloat16)

    cast(w_in, 0)
    cast(w_out, 1)
    ends = jnp.where(m == 0, 1, 0) + jnp.where(m == members - 1, 1, 0)
    pl.semaphore_wait(barrier, 6 - ends)

    def remote(src, dst, send, recv, device):
        return pltpu.make_async_remote_copy(
            src_ref=src, dst_ref=dst, send_sem=send, recv_sem=recv, device_id=device, device_id_type=MESH
        )

    def gather_copies(source, dest, base):
        first = []
        lower, upper = pl.ds(0, rhalf), pl.ds(rhalf, rhalf)
        for i, (t, part) in enumerate(((1, lower), (2, upper), (1, upper), (2, lower))):
            first.append(remote(source.at[part], dest.at[t, part], g_send.at[base + i], g_recv.at[base + i], peer(t)))
        fwd = [
            remote(dest.at[1, lower], dest.at[3, lower], g_send.at[base + 4], g_recv.at[base + 4], peer(2)),
            remote(dest.at[2, upper], dest.at[3, upper], g_send.at[base + 5], g_recv.at[base + 5], peer(1)),
        ]
        return first, fwd

    tok_first, tok_fwd = gather_copies(tok, tok_all, 0)
    cot_first, cot_fwd = gather_copies(cot, cot_all, 6)
    gate_copies = [
        remote(gates.at[t], gate_all.at[t - 1], g_send.at[11 + t], g_recv.at[11 + t], peer(t)) for t in (1, 2, 3)
    ]
    for copy in tok_first[:2]:
        copy.start()
    for copy in gate_copies:
        copy.start()
    for copy in tok_first[2:]:
        copy.start()
    tok_local = pltpu.make_async_copy(tok, tok_all.at[0], l_sem.at[0])
    cot_local = pltpu.make_async_copy(cot, cot_all.at[0], l_sem.at[1])
    tok_local.start()
    cot_local.start()

    def z_copy(way, r, k):
        return remote(
            out_z.at[way, r, k], in_z.at[way, r, k], z_send.at[way, r, k], z_recv.at[way, r, k], (up, down)[way]
        )

    def pump(r, k):
        for way in (0, 1):
            behind, ahead = (has_down, has_up) if way == 0 else (has_up, has_down)

            @pl.when(behind)
            def _():
                z_copy(way, r, k).wait_recv()

            @pl.when(behind & ahead)
            def _():
                out_z[way, r, k] = lax.select(flags[r, way] == 1, own[k], in_z[way, r, k])

            @pl.when(jnp.logical_not(behind) & ahead)
            def _():
                out_z[way, r, k] = own[k]

            @pl.when(ahead)
            def _():
                z_copy(way, r, k).start()

    def pump_all(first, last):
        for r in range(rounds):
            def step(k, carry):
                pump(r, k)
                return carry
            lax.fori_loop(first, last, step, 0)

    def started(k, mine):
        value = mine
        for r in range(rounds):
            for way in (0, 1):
                behind = has_down if way == 0 else has_up
                value = lax.select(
                    (flags[r, 2 + way] == 1) & behind, in_z[way, r, k].astype(value.dtype), value
                )
        return value

    for way in (0, 1):
        behind = has_down if way == 0 else has_up

        @pl.when(jnp.logical_not(behind))
        def _():
            for r in range(rounds):
                def clear(k, carry):
                    in_z[way, r, k] = jnp.zeros((crow, hid), jnp.bfloat16)
                    return carry
                lax.fori_loop(0, n_chunk, clear, 0)

    pump_all(0, PARTS)
    cast(m_in, 2)
    cast(s_in, 3)
    cast(m_out, 4)
    cast(s_out, 5)
    for i in (0, 1):
        tok_first[i].wait_recv()
        tok_fwd[i].start()
    for copy in cot_first:
        copy.start()
    pump_all(PARTS, 2 * PARTS)

    pair_w = []
    for i, full in enumerate((full_in, full_out)):
        for part in range(PARTS):
            k = i * PARTS + part
            full[c, pl.ds(part * crow, crow), :] = started(k, own[k])
        pair_w.append(remote(full.at[c], full.at[c], w_send.at[i], w_recv.at[i], core_peer))
        pair_w[i].start()

    pump_all(2 * PARTS, 2 * PARTS + 1)
    for copy in tok_first[2:] + tok_fwd:
        copy.wait_recv()
    tok_local.wait()
    for copy in gate_copies:
        copy.wait_recv()
    for copy in pair_w:
        copy.wait_recv()

    def gate_of(t):
        return (gates[0] if t == 0 else gate_all[t - 1]).astype(jnp.float32)

    for i in (0, 1):
        cot_first[i].wait_recv()
        cot_fwd[i].start()

    for t in range(4):
        total = jnp.dot(tok_all[t, :, pl.ds(0, half)], full_in[0], preferred_element_type=jnp.float32)
        total += jnp.dot(tok_all[t, :, pl.ds(half, half)], full_in[1], preferred_element_type=jnp.float32)
        x = total * scale_model
        pre_s[pl.ds(t * rows, rows), :] = x
        hidden = (0.5 * x * (1.0 + gelu_tanh(x))).astype(jnp.bfloat16)
        hid_s[pl.ds(t * rows, rows), :] = hidden
        gated_s[pl.ds(t * rows, rows), :] = (gate_of(t) * hidden.astype(jnp.float32)).astype(jnp.bfloat16)

    ctile = half // 2

    def layer_part(t, store):
        gate = gate_of(t)[:, 0:1]

        def step(i, carry):
            for side in (0, 1):
                wt = full_out[side, pl.ds(pl.multiple_of(i * ctile, ctile), ctile), :]
                out = lax.dot_general(
                    hid_s[pl.ds(t * rows, rows), :], wt, (((1,), (1,)), ((), ())), preferred_element_type=jnp.float32
                )
                out = (out * scale_hidden).astype(jnp.bfloat16).astype(jnp.float32) * gate
                store(side, pl.ds(pl.multiple_of(i * ctile, ctile), ctile), out)
            return carry

        lax.fori_loop(0, 2, step, 0)

    def store_diag(side, cols, out):
        (send_a, send_b)[side][1, :, cols] = out.astype(jnp.bfloat16)

    def store_first(side, cols, out):
        if side == 0:
            send_a[0, :, cols] = out.astype(jnp.bfloat16)
        else:
            keep_b[:, cols] = out

    def store_second(side, cols, out):
        if side == 1:
            send_b[0, :, cols] = out.astype(jnp.bfloat16)
        else:
            keep_a[:, cols] = out

    def store_own(side, cols, out):
        own_part[side, :, cols] = out

    layer_part(3, store_diag)
    ret1 = [
        remote(send_a.at[1], got_a.at[1], r_send.at[0], r_recv.at[0], peer(1)),
        remote(send_b.at[1], got_b.at[1], r_send.at[1], r_recv.at[1], peer(2)),
        remote(send_a.at[0], got_a.at[0], r_send.at[2], r_recv.at[2], peer(1)),
        remote(send_b.at[0], got_b.at[0], r_send.at[3], r_recv.at[3], peer(2)),
    ]
    ret2 = [
        remote(send2.at[0], got2.at[0], r_send.at[4], r_recv.at[4], peer(2)),
        remote(send2.at[1], got2.at[1], r_send.at[5], r_recv.at[5], peer(1)),
    ]
    ret1[0].start()
    ret1[1].start()
    layer_part(1, store_first)
    ret1[2].start()
    layer_part(2, store_second)
    ret1[3].start()
    layer_part(0, store_own)
    pump_all(2 * PARTS + 1, 2 * PARTS + 4)

    cot_local.wait()
    for copy in cot_first[2:] + cot_fwd:
        copy.wait_recv()

    for t in range(4):
        total = jnp.dot(cot_all[t, :, pl.ds(0, half)], full_out[0], preferred_element_type=jnp.float32)
        total += jnp.dot(cot_all[t, :, pl.ds(half, half)], full_out[1], preferred_element_type=jnp.float32)
        upstream = total * scale_hidden * gate_of(t)
        x = pre_s[pl.ds(t * rows, rows), :]
        th = gelu_tanh(x)
        slope = 0.5 * (1.0 + th) + 0.5 * x * (1.0 - th * th) * (GELU_C * (1.0 + 3.0 * GELU_A * x * x))
        back_s[pl.ds(t * rows, rows), :] = (upstream * slope).astype(jnp.bfloat16)

    gtile = half // 4

    def gradient(source, right, scale, side, i):
        cols = pl.ds(pl.multiple_of(side * half + i * gtile, gtile), gtile)
        left = source[:, :, cols].reshape(4 * rows, gtile)
        return lax.dot_general(
            left, right[...], (((0,), (0,)), ((), ())), preferred_element_type=jnp.float32
        ) * scale

    plan = ((cot_all, gated_s, scale_hidden, 1), (tok_all, back_s, scale_model, 0))
    pair_g = []
    for source, right, scale, which in plan:
        def give(i, carry):
            grad_send[which, pl.ds(pl.multiple_of(i * gtile, gtile), gtile), :] = gradient(
                source, right, scale, 1 - c, i
            ).astype(jnp.bfloat16)
            return carry
        lax.fori_loop(0, 4, give, 0)
        copy = remote(grad_send.at[which], grad_got.at[which], d_send.at[which], d_recv.at[which], core_peer)
        copy.start()
        pair_g.append(copy)
    for source, right, scale, which in plan:
        def keep(i, carry):
            grad_own[which, pl.ds(pl.multiple_of(i * gtile, gtile), gtile), :] = gradient(source, right, scale, c, i)
            return carry
        lax.fori_loop(0, 4, keep, 0)

    pump_all(2 * PARTS + 4, n_chunk)

    ret1[0].wait_recv()
    send2[0] = (keep_a[...] + got_a[1].astype(jnp.float32)).astype(jnp.bfloat16)
    ret2[0].start()
    ret1[1].wait_recv()
    send2[1] = (keep_b[...] + got_b[1].astype(jnp.float32)).astype(jnp.bfloat16)
    ret2[1].start()

    for copy in pair_g:
        copy.wait_recv()
    rate = rate_ref[0]
    for which, full, first, second, out in ((0, full_in, m_in, s_in, new_in), (1, full_out, m_out, s_out, new_out)):
        for part in range(PARTS):
            span = pl.ds(part * crow, crow)
            grad = grad_own[which, span, :] + grad_got[which, span, :].astype(jnp.float32)
            f = started((2 + 2 * which) * PARTS + part, first[span, :])
            s = started((3 + 2 * which) * PARTS + part, second[span, :])
            f_new = beta_first * f + (1.0 - beta_first) * grad
            s_new = beta_second * s + (1.0 - beta_second) * grad * grad
            start = full[c, span, :].astype(jnp.float32)
            out[span, :] = (start - rate * f_new / (jnp.sqrt(s_new) + adam_floor)).astype(jnp.bfloat16)

    for copy in ret1[2:] + ret2:
        copy.wait_recv()
    layer_out[:, pl.ds(0, half)] = (
        own_part[0] + got_a[0].astype(jnp.float32) + got2[0].astype(jnp.float32)
    ).astype(jnp.bfloat16)
    layer_out[:, pl.ds(half, half)] = (
        own_part[1] + got_b[0].astype(jnp.float32) + got2[1].astype(jnp.float32)
    ).astype(jnp.bfloat16)

    for copy in tok_first + tok_fwd + cot_first + cot_fwd + gate_copies + pair_w + ret1 + ret2 + pair_g:
        copy.wait_send()
    for r in range(rounds):
        for way in (0, 1):
            ahead = has_up if way == 0 else has_down

            @pl.when(ahead)
            def _():
                def drain(k, carry):
                    z_copy(way, r, k).wait_send()
                    return carry
                lax.fori_loop(0, n_chunk, drain, 0)


def fused_call(rounds, members, arrays):
    tokens, w_in = arrays[2], arrays[5]
    rows, width = tokens.shape
    wrows, hid = w_in.shape
    half = width // 2
    crow = wrows // PARTS
    n_chunk = 6 * PARTS
    bf, f32 = jnp.bfloat16, jnp.float32
    vmem = pl.BlockSpec(memory_space=pltpu.VMEM)
    smem = pl.BlockSpec(memory_space=pltpu.SMEM)
    dma = pltpu.SemaphoreType.DMA
    return pl.pallas_call(
        functools.partial(fused_kernel, rounds, members),
        out_shape=(
            jax.ShapeDtypeStruct((wrows, hid), bf),
            jax.ShapeDtypeStruct((wrows, hid), bf),
            jax.ShapeDtypeStruct((rows, width), bf),
        ),
        in_specs=[smem] * 2 + [vmem] * 9,
        out_specs=(vmem,) * 3,
        scratch_shapes=[
            pltpu.VMEM((n_chunk, crow, hid), bf),
            pltpu.VMEM((2, rounds, n_chunk, crow, hid), bf),
            pltpu.VMEM((2, rounds, n_chunk, crow, hid), bf),
            pltpu.VMEM((4, rows, width), bf),
            pltpu.VMEM((4, rows, width), bf),
            pltpu.VMEM((3, rows, hid), bf),
            pltpu.VMEM((2, wrows, hid), bf),
            pltpu.VMEM((2, wrows, hid), bf),
            pltpu.VMEM((4 * rows, hid), f32),
            pltpu.VMEM((4 * rows, hid), bf),
            pltpu.VMEM((4 * rows, hid), bf),
            pltpu.VMEM((4 * rows, hid), bf),
            pltpu.VMEM((2, rows, half), f32),
            pltpu.VMEM((rows, half), f32),
            pltpu.VMEM((rows, half), f32),
            pltpu.VMEM((2, rows, half), bf),
            pltpu.VMEM((2, rows, half), bf),
            pltpu.VMEM((2, rows, half), bf),
            pltpu.VMEM((2, rows, half), bf),
            pltpu.VMEM((2, rows, half), bf),
            pltpu.VMEM((2, rows, half), bf),
            pltpu.VMEM((2, wrows, hid), f32),
            pltpu.VMEM((2, wrows, hid), bf),
            pltpu.VMEM((2, wrows, hid), bf),
            dma((2, rounds, n_chunk)),
            dma((2, rounds, n_chunk)),
            dma((1,)),
            dma((1,)),
            dma((15,)),
            dma((15,)),
            dma((2,)),
            dma((2,)),
            dma((6,)),
            dma((6,)),
            dma((2,)),
            dma((2,)),
            dma((2,)),
        ],
        compiler_params=pltpu.CompilerParams(
            collective_id=rounds - 1, has_side_effects=True, vmem_limit_bytes=56 * 1024 * 1024
        ),
    )(*arrays)


def on_device_fused(
    tokens, cotangent, routes, gate_probs, weight_in, weight_out, moment_in, square_in,
    moment_out, square_out, parents, own_rates, perturbed,
):
    members = lax.axis_size("member") // 2
    member = lax.axis_index("member") // 2
    expert = lax.axis_index("expert")
    ids = jnp.arange(members, dtype=jnp.int32)
    copies = parents != ids
    rate = jnp.sum(jnp.where(ids == member, jnp.where(copies, perturbed, own_rates), 0.0)).reshape(1)
    hid = weight_in.shape[1]
    named = jnp.stack([expert // 2 * 2 + expert % 2, expert // 2 * 2 + 1 - expert % 2,
                       (1 - expert // 2) * 2 + expert % 2, (1 - expert // 2) * 2 + 1 - expert % 2])
    table = jnp.sum(
        jnp.where(routes[None, :, :] == named[:, None, None], gate_probs.astype(jnp.float32)[None], 0.0), axis=2
    )
    gates = jnp.broadcast_to(table[:, :, None].astype(jnp.bfloat16), (4, tokens.shape[0], hid))
    link = ids[:, None]
    right_use = jnp.sum(copies[None] & (ids[None] > link) & (parents[None] <= link), axis=1)
    left_use = jnp.sum(copies[None] & (ids[None] <= link) & (parents[None] > link), axis=1)
    crowded = jnp.maximum(jnp.max(right_use), jnp.max(left_use)) > 1
    order = jnp.sum((copies[None, :] & (ids[None, :] < ids[:, None])).astype(jnp.int32), axis=1)

    def flags_for(rounds):
        rows = []
        for r in range(rounds):
            mine = copies & (order % rounds == r)
            rows.append(jnp.stack([
                jnp.any(mine & (parents == member) & (ids > member)),
                jnp.any(mine & (parents == member) & (ids < member)),
                jnp.any(mine & (ids == member) & (parents < member)),
                jnp.any(mine & (ids == member) & (parents > member)),
            ]))
        return jnp.stack(rows).astype(jnp.int32)

    rest = (rate, tokens, cotangent, gates, weight_in, weight_out, moment_in, square_in, moment_out, square_out)
    return lax.cond(
        crowded,
        lambda: tuple(fused_call(2, members, (flags_for(2), *rest))),
        lambda: tuple(fused_call(1, members, (flags_for(1), *rest))),
    )


def solution(mesh):
    fused = mesh.shape["member"] // 4 <= 2 and mesh.shape["expert"] == 4
    in_specs = (
        P(("member", "expert"), None),
        P(("member", "expert"), None),
        P(("member", "expert"), None),
        P(("member", "expert"), None),
        P("member", "expert"),
        P("member", "expert"),
        P("member", "expert"),
        P("member", "expert"),
        P("member", "expert"),
        P("member", "expert"),
        P(),
        P(),
        P(),
    )
    out_specs = (P("member", "expert"), P("member", "expert"), P(("member", "expert"), None))
    return jax.shard_map(
        on_device_fused if fused else on_device, mesh=mesh, in_specs=in_specs, out_specs=out_specs, check_vma=False
    )
```

```python
import functools

import jax
import jax.numpy as jnp
from jax import lax
from jax.experimental import pallas as pl
from jax.experimental.pallas import tpu as pltpu
from jax.sharding import PartitionSpec as P

beta_first = 0.9
beta_second = 0.999
adam_floor = 1e-08


def for_sending(shard):

    def short(part):
        return part.astype(jnp.bfloat16) if part.dtype == jnp.float32 else part

    return jax.tree.map(short, shard)


def partner(shard, axis, bit):
    return lax.ppermute(shard, axis, [(i, i ^ 1 << bit) for i in range(lax.axis_size(axis))])


def gelu_back(pre_act, upstream):
    _, pullback = jax.vjp(lambda inner: jax.nn.gelu(inner, approximate=True), pre_act)
    return pullback(upstream)[0]


def adam_step(param, moment, square, gradient, step_rate):
    moment_new = beta_first * moment + (1.0 - beta_first) * gradient
    square_new = beta_second * square + (1.0 - beta_second) * gradient * gradient
    moved = param.astype(jnp.float32) - step_rate * moment_new / (jnp.sqrt(square_new) + adam_floor)
    return moved.astype(jnp.bfloat16)


def pick_rows(pieces, choose):
    return tuple((jnp.take(piece, choose, axis=0) for piece in pieces))


def relay_together(arrays, choose, devices):
    flat = [array.reshape(devices, -1) for array in arrays]
    sent = (
        lax.all_to_all(
            flat[0].astype(jnp.bfloat16), "member", split_axis=0, concat_axis=0, tiled=True
        ).astype(jnp.float32),
        lax.all_to_all(
            flat[1].astype(jnp.bfloat16), "member", split_axis=0, concat_axis=0, tiled=True
        ).astype(jnp.float32),
        lax.all_to_all(
            flat[2].astype(jnp.bfloat16), "member", split_axis=0, concat_axis=0, tiled=True
        ).astype(jnp.float32),
        lax.all_to_all(
            flat[3].astype(jnp.bfloat16), "member", split_axis=0, concat_axis=0, tiled=True
        ).astype(jnp.float32),
        lax.all_to_all(
            flat[4].astype(jnp.bfloat16), "member", split_axis=0, concat_axis=0, tiled=True
        ).astype(jnp.float32),
        lax.all_to_all(
            flat[5].astype(jnp.bfloat16), "member", split_axis=0, concat_axis=0, tiled=True
        ).astype(jnp.float32),
    )
    picked = pick_rows(sent, choose)
    landed = (
        lax.all_to_all(for_sending(picked[0]), "member", split_axis=0, concat_axis=0, tiled=True),
        lax.all_to_all(for_sending(picked[1]), "member", split_axis=0, concat_axis=0, tiled=True),
        lax.all_to_all(for_sending(picked[2]), "member", split_axis=0, concat_axis=0, tiled=True),
        lax.all_to_all(for_sending(picked[3]), "member", split_axis=0, concat_axis=0, tiled=True),
        lax.all_to_all(for_sending(picked[4]), "member", split_axis=0, concat_axis=0, tiled=True),
        lax.all_to_all(for_sending(picked[5]), "member", split_axis=0, concat_axis=0, tiled=True),
    )
    return [piece.reshape(array.shape) for piece, array in zip(landed, arrays)]


def train_pass(start_in, start_out, tokens, cotangent, routes, gate_probs, upper_half):
    half_rows = start_in.shape[0]
    width = tokens.shape[1]
    scale_model = width ** (-0.5)
    scale_hidden = start_in.shape[1] ** (-0.5)
    partner_in, partner_out = partner((start_in, start_out), "member", 0)
    is_upper = upper_half == 1
    full_in = jnp.where(
        is_upper,
        jnp.concatenate([partner_in, start_in], 0),
        jnp.concatenate([start_in, partner_in], 0),
    )
    full_out = jnp.where(
        is_upper,
        jnp.concatenate([partner_out, start_out], 0),
        jnp.concatenate([start_out, partner_out], 0),
    )
    experts = lax.axis_size("expert")
    tok_rows = tokens.shape[0]
    capacity = min(tok_rows, 5 * tok_rows // experts)
    flat_route = routes.reshape(-1)
    expert_ids = jnp.arange(experts, dtype=jnp.int32)
    onehot = (flat_route[:, None] == expert_ids[None, :]).astype(jnp.int32)
    places = jnp.arange(flat_route.shape[0], dtype=jnp.int32)
    before = (places[None, :] < places[:, None]).astype(jnp.float32)
    earlier = jnp.dot(before, onehot.astype(jnp.float32)).astype(jnp.int32)
    position_in = jnp.sum(earlier * onehot, axis=1)
    slot_of = flat_route * capacity + position_in
    slot_ids = jnp.arange(experts * capacity, dtype=jnp.int32)
    pairing = slot_of[None, :] == slot_ids[:, None]
    filled = jnp.any(pairing, axis=1)
    assign_ids = jnp.arange(flat_route.shape[0], dtype=jnp.int32)
    assigned = jnp.sum(jnp.where(pairing, assign_ids[None, :], 0), axis=1)
    token_of = jnp.where(filled, assigned // 2, tok_rows)
    zero_row = jnp.zeros((1, width), jnp.bfloat16)
    send_tokens = jnp.take(jnp.concatenate([tokens, zero_row], 0), token_of, axis=0).reshape(
        experts, capacity, width
    )
    send_cotan = jnp.take(jnp.concatenate([cotangent, zero_row], 0), token_of, axis=0).reshape(
        experts, capacity, width
    )
    send_gates = jnp.where(
        filled, jnp.take(gate_probs.reshape(-1), assigned), jnp.zeros((), jnp.bfloat16)
    ).reshape(experts, capacity)
    got_tokens, got_cotan, got_gates = (
        lax.all_to_all(send_tokens, "expert", split_axis=0, concat_axis=0, tiled=True),
        lax.all_to_all(send_cotan, "expert", split_axis=0, concat_axis=0, tiled=True),
        lax.all_to_all(send_gates, "expert", split_axis=0, concat_axis=0, tiled=True),
    )
    rows_tokens = got_tokens.reshape(-1, width)
    rows_cotan = got_cotan.reshape(-1, width)
    rows_gates = got_gates.reshape(-1, 1).astype(jnp.float32)
    pre_act = jnp.dot(rows_tokens, full_in, preferred_element_type=jnp.float32) * scale_model
    hidden = jax.nn.gelu(pre_act, approximate=True).astype(jnp.bfloat16)
    expert_out = (
        lax.dot_general(
            hidden, full_out, (((1,), (1,)), ((), ())), preferred_element_type=jnp.float32
        )
        * scale_hidden
    ).astype(jnp.bfloat16)
    returned = lax.all_to_all(
        expert_out.reshape(experts, capacity, width),
        "expert",
        split_axis=0,
        concat_axis=0,
        tiled=True,
    )
    gathered = jnp.take(returned.reshape(-1, width), slot_of, axis=0).reshape(tok_rows, 2, width)
    weighted = gathered.astype(jnp.float32) * gate_probs.astype(jnp.float32)[:, :, None]
    layer_out = (weighted[:, 0] + weighted[:, 1]).astype(jnp.bfloat16)
    gated_hidden = (rows_gates * hidden.astype(jnp.float32)).astype(jnp.bfloat16)
    grad_out_full = (
        lax.dot_general(
            rows_cotan, gated_hidden, (((0,), (0,)), ((), ())), preferred_element_type=jnp.float32
        )
        * scale_hidden
    )
    back_hidden = (
        jnp.dot(rows_cotan, full_out, preferred_element_type=jnp.float32)
        * scale_hidden
        * rows_gates
    )
    back_pre = gelu_back(pre_act, back_hidden).astype(jnp.bfloat16)
    grad_in_full = (
        lax.dot_general(
            rows_tokens, back_pre, (((0,), (0,)), ((), ())), preferred_element_type=jnp.float32
        )
        * scale_model
    )
    other_start = (1 - upper_half) * half_rows
    own_start = upper_half * half_rows
    give_in = lax.dynamic_slice_in_dim(grad_in_full, other_start, half_rows, 0)
    give_out = lax.dynamic_slice_in_dim(grad_out_full, other_start, half_rows, 0)
    taken_in, taken_out = (
        partner(give_in.astype(jnp.bfloat16), "member", 0).astype(give_in.dtype),
        partner(give_out.astype(jnp.bfloat16), "member", 0).astype(give_out.dtype),
    )
    grad_in = lax.dynamic_slice_in_dim(grad_in_full, own_start, half_rows, 0) + taken_in
    grad_out = lax.dynamic_slice_in_dim(grad_out_full, own_start, half_rows, 0) + taken_out
    return (grad_in, grad_out, layer_out)


def on_device(
    tokens,
    cotangent,
    routes,
    gate_probs,
    weight_in,
    weight_out,
    moment_in,
    square_in,
    moment_out,
    square_out,
    parents,
    own_rates,
    perturbed,
):
    devices = lax.axis_size("member")
    position = lax.axis_index("member")
    member = position // 2
    upper_half = position % 2
    member_ids = jnp.arange(parents.shape[0], dtype=jnp.int32)
    device_ids = jnp.arange(devices, dtype=jnp.int32)
    from_device = 2 * jnp.take(parents, device_ids // 2) + device_ids % 2
    chosen_rates = jnp.where(parents != member_ids, perturbed, own_rates)
    own_rate = jnp.take(chosen_rates, member)
    landed = relay_together(
        (
            weight_in.astype(jnp.float32),
            weight_out.astype(jnp.float32),
            moment_in,
            square_in,
            moment_out,
            square_out,
        ),
        from_device,
        devices,
    )
    start_in = landed[0].astype(jnp.bfloat16)
    start_out = landed[1].astype(jnp.bfloat16)
    grad_in, grad_out, layer_out = train_pass(
        start_in, start_out, tokens, cotangent, routes, gate_probs, upper_half
    )
    new_in = adam_step(start_in, landed[2], landed[3], grad_in, own_rate)
    new_out = adam_step(start_out, landed[4], landed[5], grad_out, own_rate)
    return (new_in, new_out, layer_out)


MESH = pl.DeviceIdType.MESH
PARTS = 2
GELU_C = 0.7978845608028654
GELU_A = 0.044715


def gelu_tanh(x):
    return jnp.tanh(GELU_C * (x + GELU_A * x * x * x))


def fused_kernel(rounds, members, *refs):
    (flags, rate_ref, tok, cot, gates, w_in, w_out, m_in, s_in, m_out, s_out,
     new_in, new_out, layer_out,
     own, in_z, out_z, tok_all, cot_all, gate_all, full_in, full_out,
     pre_s, hid_s, gated_s, back_s, own_part, keep_a, keep_b, send_a, send_b, got_a, got_b,
     send2, got2, grad_own, grad_send, grad_got,
     z_send, z_recv, p_send, p_recv, g_send, g_recv, w_send, w_recv, r_send, r_recv, d_send, d_recv, l_sem,
     ) = refs
    position = lax.axis_index("member")
    expert = lax.axis_index("expert")
    m = position // 2
    c = position % 2
    ex, ey = expert % 2, expert // 2
    rows, width = tok.shape
    half = width // 2
    rhalf = rows // 2
    wrows, hid = w_in.shape
    crow = wrows // PARTS
    n_chunk = 6 * PARTS
    scale_model = width ** (-0.5)
    scale_hidden = hid ** (-0.5)

    def peer(t):
        return {"expert": ((ey + t // 2) % 2) * 2 + (ex + t % 2) % 2}

    core_peer = {"member": m * 2 + (1 - c)}
    up = {"member": lax.rem(m + 1, members) * 2 + c}
    down = {"member": lax.rem(m + members - 1, members) * 2 + c}
    has_up = m < members - 1
    has_down = m > 0

    barrier = pltpu.get_barrier_semaphore()
    for t in (1, 2, 3):
        pl.semaphore_signal(barrier, inc=1, device_id=peer(t), device_id_type=MESH)
    pl.semaphore_signal(barrier, inc=1, device_id=core_peer, device_id_type=MESH)

    @pl.when(has_up)
    def _():
        pl.semaphore_signal(barrier, inc=1, device_id=up, device_id_type=MESH)

    @pl.when(has_down)
    def _():
        pl.semaphore_signal(barrier, inc=1, device_id=down, device_id_type=MESH)

    def cast(source, index):
        for part in range(PARTS):
            own[index * PARTS + part] = source[pl.ds(part * crow, crow), :].astype(jnp.bfloat16)

    cast(w_in, 0)
    cast(w_out, 1)
    ends = jnp.where(m == 0, 1, 0) + jnp.where(m == members - 1, 1, 0)
    pl.semaphore_wait(barrier, 6 - ends)

    def remote(src, dst, send, recv, device):
        return pltpu.make_async_remote_copy(
            src_ref=src, dst_ref=dst, send_sem=send, recv_sem=recv, device_id=device, device_id_type=MESH
        )

    def gather_copies(source, dest, base):
        first = []
        lower, upper = pl.ds(0, rhalf), pl.ds(rhalf, rhalf)
        for i, (t, part) in enumerate(((1, lower), (2, upper), (1, upper), (2, lower))):
            first.append(remote(source.at[part], dest.at[t, part], g_send.at[base + i], g_recv.at[base + i], peer(t)))
        fwd = [
            remote(dest.at[1, lower], dest.at[3, lower], g_send.at[base + 4], g_recv.at[base + 4], peer(2)),
            remote(dest.at[2, upper], dest.at[3, upper], g_send.at[base + 5], g_recv.at[base + 5], peer(1)),
        ]
        return first, fwd

    tok_first, tok_fwd = gather_copies(tok, tok_all, 0)
    cot_first, cot_fwd = gather_copies(cot, cot_all, 6)
    gate_copies = [
        remote(gates.at[t], gate_all.at[t - 1], g_send.at[11 + t], g_recv.at[11 + t], peer(t)) for t in (1, 2, 3)
    ]
    for copy in tok_first[:2]:
        copy.start()
    for copy in gate_copies:
        copy.start()
    for copy in tok_first[2:]:
        copy.start()
    tok_local = pltpu.make_async_copy(tok, tok_all.at[0], l_sem.at[0])
    cot_local = pltpu.make_async_copy(cot, cot_all.at[0], l_sem.at[1])
    tok_local.start()
    cot_local.start()

    def z_copy(way, r, k):
        return remote(
            out_z.at[way, r, k], in_z.at[way, r, k], z_send.at[way, r, k], z_recv.at[way, r, k], (up, down)[way]
        )

    def forward(way, r, k):
        behind, ahead = (has_down, has_up) if way == 0 else (has_up, has_down)

        @pl.when(behind)
        def _():
            z_copy(way, r, k).wait_recv()

        @pl.when(behind & ahead)
        def _():
            out_z[way, r, k] = lax.select(flags[r, way] == 1, own[k], in_z[way, r, k])
            z_copy(way, r, k).start()

    def pump(r, k):
        @pl.when(m < members // 2)
        def _():
            forward(0, r, k)
            forward(1, r, k)

        @pl.when(m >= members // 2)
        def _():
            forward(1, r, k)
            forward(0, r, k)

    def pump_all(first, last):
        for r in range(rounds):
            def step(k, carry):
                pump(r, k)
                return carry
            lax.fori_loop(first, last, step, 0)

    def started(k, mine):
        value = mine
        for r in range(rounds):
            for way in (0, 1):
                behind = has_down if way == 0 else has_up
                value = lax.select(
                    (flags[r, 2 + way] == 1) & behind, in_z[way, r, k].astype(value.dtype), value
                )
        return value

    def launch(first, last):
        for way in (0, 1):
            behind, ahead = (has_down, has_up) if way == 0 else (has_up, has_down)
            for r in range(rounds):
                @pl.when(jnp.logical_not(behind) & ahead)
                def _():
                    def step(k, carry):
                        out_z[way, r, k] = own[k]
                        z_copy(way, r, k).start()
                        return carry
                    lax.fori_loop(first, last, step, 0)

    launch(0, 2 * PARTS)
    cast(m_in, 2)
    cast(s_in, 3)
    cast(m_out, 4)
    cast(s_out, 5)
    launch(2 * PARTS, n_chunk)

    for way in (0, 1):
        behind = has_down if way == 0 else has_up

        @pl.when(jnp.logical_not(behind))
        def _():
            for r in range(rounds):
                def clear(k, carry):
                    in_z[way, r, k] = jnp.zeros((crow, hid), jnp.bfloat16)
                    return carry
                lax.fori_loop(0, n_chunk, clear, 0)

    pump_all(0, PARTS)
    for i in (0, 1):
        tok_first[i].wait_recv()
        tok_fwd[i].start()
    for copy in cot_first:
        copy.start()
    pump_all(PARTS, 2 * PARTS)

    pair_w = []
    for i, full in enumerate((full_in, full_out)):
        for part in range(PARTS):
            k = i * PARTS + part
            full[c, pl.ds(part * crow, crow), :] = started(k, own[k])
        pair_w.append(remote(full.at[c], full.at[c], w_send.at[i], w_recv.at[i], core_peer))
        pair_w[i].start()

    pump_all(2 * PARTS, 2 * PARTS + 1)
    for copy in tok_first[2:] + tok_fwd:
        copy.wait_recv()
    tok_local.wait()
    for copy in gate_copies:
        copy.wait_recv()
    for copy in pair_w:
        copy.wait_recv()

    def gate_of(t):
        return (gates[0] if t == 0 else gate_all[t - 1]).astype(jnp.float32)

    for i in (0, 1):
        cot_first[i].wait_recv()
        cot_fwd[i].start()

    for t in range(4):
        total = jnp.dot(tok_all[t, :, pl.ds(0, half)], full_in[0], preferred_element_type=jnp.float32)
        total += jnp.dot(tok_all[t, :, pl.ds(half, half)], full_in[1], preferred_element_type=jnp.float32)
        x = total * scale_model
        pre_s[pl.ds(t * rows, rows), :] = x
        hidden = (0.5 * x * (1.0 + gelu_tanh(x))).astype(jnp.bfloat16)
        hid_s[pl.ds(t * rows, rows), :] = hidden
        gated_s[pl.ds(t * rows, rows), :] = (gate_of(t) * hidden.astype(jnp.float32)).astype(jnp.bfloat16)

    ctile = half // 2

    def layer_part(t, store):
        gate = gate_of(t)[:, 0:1]

        def step(i, carry):
            for side in (0, 1):
                wt = full_out[side, pl.ds(pl.multiple_of(i * ctile, ctile), ctile), :]
                out = lax.dot_general(
                    hid_s[pl.ds(t * rows, rows), :], wt, (((1,), (1,)), ((), ())), preferred_element_type=jnp.float32
                )
                out = (out * scale_hidden).astype(jnp.bfloat16).astype(jnp.float32) * gate
                store(side, pl.ds(pl.multiple_of(i * ctile, ctile), ctile), out)
            return carry

        lax.fori_loop(0, 2, step, 0)

    def store_diag(side, cols, out):
        (send_a, send_b)[side][1, :, cols] = out.astype(jnp.bfloat16)

    def store_first(side, cols, out):
        if side == 0:
            send_a[0, :, cols] = out.astype(jnp.bfloat16)
        else:
            keep_b[:, cols] = out

    def store_second(side, cols, out):
        if side == 1:
            send_b[0, :, cols] = out.astype(jnp.bfloat16)
        else:
            keep_a[:, cols] = out

    def store_own(side, cols, out):
        own_part[side, :, cols] = out

    layer_part(3, store_diag)
    ret1 = [
        remote(send_a.at[1], got_a.at[1], r_send.at[0], r_recv.at[0], peer(1)),
        remote(send_b.at[1], got_b.at[1], r_send.at[1], r_recv.at[1], peer(2)),
        remote(send_a.at[0], got_a.at[0], r_send.at[2], r_recv.at[2], peer(1)),
        remote(send_b.at[0], got_b.at[0], r_send.at[3], r_recv.at[3], peer(2)),
    ]
    ret2 = [
        remote(send2.at[0], got2.at[0], r_send.at[4], r_recv.at[4], peer(2)),
        remote(send2.at[1], got2.at[1], r_send.at[5], r_recv.at[5], peer(1)),
    ]
    ret1[0].start()
    ret1[1].start()
    layer_part(1, store_first)
    ret1[2].start()
    layer_part(2, store_second)
    ret1[3].start()
    layer_part(0, store_own)
    pump_all(2 * PARTS + 1, 2 * PARTS + 4)

    cot_local.wait()
    for copy in cot_first[2:] + cot_fwd:
        copy.wait_recv()

    for t in range(4):
        total = jnp.dot(cot_all[t, :, pl.ds(0, half)], full_out[0], preferred_element_type=jnp.float32)
        total += jnp.dot(cot_all[t, :, pl.ds(half, half)], full_out[1], preferred_element_type=jnp.float32)
        upstream = total * scale_hidden * gate_of(t)
        x = pre_s[pl.ds(t * rows, rows), :]
        th = gelu_tanh(x)
        slope = 0.5 * (1.0 + th) + 0.5 * x * (1.0 - th * th) * (GELU_C * (1.0 + 3.0 * GELU_A * x * x))
        back_s[pl.ds(t * rows, rows), :] = (upstream * slope).astype(jnp.bfloat16)

    gtile = half // 4

    def gradient(source, right, scale, side, i):
        cols = pl.ds(pl.multiple_of(side * half + i * gtile, gtile), gtile)
        left = source[:, :, cols].reshape(4 * rows, gtile)
        return lax.dot_general(
            left, right[...], (((0,), (0,)), ((), ())), preferred_element_type=jnp.float32
        ) * scale

    plan = ((cot_all, gated_s, scale_hidden, 1), (tok_all, back_s, scale_model, 0))
    pair_g = []
    for source, right, scale, which in plan:
        def give(i, carry):
            grad_send[which, pl.ds(pl.multiple_of(i * gtile, gtile), gtile), :] = gradient(
                source, right, scale, 1 - c, i
            ).astype(jnp.bfloat16)
            return carry
        lax.fori_loop(0, 4, give, 0)
        copy = remote(grad_send.at[which], grad_got.at[which], d_send.at[which], d_recv.at[which], core_peer)
        copy.start()
        pair_g.append(copy)
    for source, right, scale, which in plan:
        def keep(i, carry):
            grad_own[which, pl.ds(pl.multiple_of(i * gtile, gtile), gtile), :] = gradient(source, right, scale, c, i)
            return carry
        lax.fori_loop(0, 4, keep, 0)

    pump_all(2 * PARTS + 4, n_chunk)

    ret1[0].wait_recv()
    send2[0] = (keep_a[...] + got_a[1].astype(jnp.float32)).astype(jnp.bfloat16)
    ret2[0].start()
    ret1[1].wait_recv()
    send2[1] = (keep_b[...] + got_b[1].astype(jnp.float32)).astype(jnp.bfloat16)
    ret2[1].start()

    for copy in pair_g:
        copy.wait_recv()
    rate = rate_ref[0]
    for which, full, first, second, out in ((0, full_in, m_in, s_in, new_in), (1, full_out, m_out, s_out, new_out)):
        for part in range(PARTS):
            span = pl.ds(part * crow, crow)
            grad = grad_own[which, span, :] + grad_got[which, span, :].astype(jnp.float32)
            f = started((2 + 2 * which) * PARTS + part, first[span, :])
            s = started((3 + 2 * which) * PARTS + part, second[span, :])
            f_new = beta_first * f + (1.0 - beta_first) * grad
            s_new = beta_second * s + (1.0 - beta_second) * grad * grad
            start = full[c, span, :].astype(jnp.float32)
            out[span, :] = (start - rate * f_new / (jnp.sqrt(s_new) + adam_floor)).astype(jnp.bfloat16)

    for copy in ret1[2:] + ret2:
        copy.wait_recv()
    layer_out[:, pl.ds(0, half)] = (
        own_part[0] + got_a[0].astype(jnp.float32) + got2[0].astype(jnp.float32)
    ).astype(jnp.bfloat16)
    layer_out[:, pl.ds(half, half)] = (
        own_part[1] + got_b[0].astype(jnp.float32) + got2[1].astype(jnp.float32)
    ).astype(jnp.bfloat16)

    for copy in tok_first + tok_fwd + cot_first + cot_fwd + gate_copies + pair_w + ret1 + ret2 + pair_g:
        copy.wait_send()
    for r in range(rounds):
        for way in (0, 1):
            ahead = has_up if way == 0 else has_down

            @pl.when(ahead)
            def _():
                def drain(k, carry):
                    z_copy(way, r, k).wait_send()
                    return carry
                lax.fori_loop(0, n_chunk, drain, 0)


def fused_call(rounds, members, arrays):
    tokens, w_in = arrays[2], arrays[5]
    rows, width = tokens.shape
    wrows, hid = w_in.shape
    half = width // 2
    crow = wrows // PARTS
    n_chunk = 6 * PARTS
    bf, f32 = jnp.bfloat16, jnp.float32
    vmem = pl.BlockSpec(memory_space=pltpu.VMEM)
    smem = pl.BlockSpec(memory_space=pltpu.SMEM)
    dma = pltpu.SemaphoreType.DMA
    return pl.pallas_call(
        functools.partial(fused_kernel, rounds, members),
        out_shape=(
            jax.ShapeDtypeStruct((wrows, hid), bf),
            jax.ShapeDtypeStruct((wrows, hid), bf),
            jax.ShapeDtypeStruct((rows, width), bf),
        ),
        in_specs=[smem] * 2 + [vmem] * 9,
        out_specs=(vmem,) * 3,
        scratch_shapes=[
            pltpu.VMEM((n_chunk, crow, hid), bf),
            pltpu.VMEM((2, rounds, n_chunk, crow, hid), bf),
            pltpu.VMEM((2, rounds, n_chunk, crow, hid), bf),
            pltpu.VMEM((4, rows, width), bf),
            pltpu.VMEM((4, rows, width), bf),
            pltpu.VMEM((3, rows, hid), bf),
            pltpu.VMEM((2, wrows, hid), bf),
            pltpu.VMEM((2, wrows, hid), bf),
            pltpu.VMEM((4 * rows, hid), f32),
            pltpu.VMEM((4 * rows, hid), bf),
            pltpu.VMEM((4 * rows, hid), bf),
            pltpu.VMEM((4 * rows, hid), bf),
            pltpu.VMEM((2, rows, half), f32),
            pltpu.VMEM((rows, half), f32),
            pltpu.VMEM((rows, half), f32),
            pltpu.VMEM((2, rows, half), bf),
            pltpu.VMEM((2, rows, half), bf),
            pltpu.VMEM((2, rows, half), bf),
            pltpu.VMEM((2, rows, half), bf),
            pltpu.VMEM((2, rows, half), bf),
            pltpu.VMEM((2, rows, half), bf),
            pltpu.VMEM((2, wrows, hid), f32),
            pltpu.VMEM((2, wrows, hid), bf),
            pltpu.VMEM((2, wrows, hid), bf),
            dma((2, rounds, n_chunk)),
            dma((2, rounds, n_chunk)),
            dma((1,)),
            dma((1,)),
            dma((15,)),
            dma((15,)),
            dma((2,)),
            dma((2,)),
            dma((6,)),
            dma((6,)),
            dma((2,)),
            dma((2,)),
            dma((2,)),
        ],
        compiler_params=pltpu.CompilerParams(
            collective_id=rounds - 1, has_side_effects=True, vmem_limit_bytes=56 * 1024 * 1024
        ),
    )(*arrays)


def on_device_fused(
    tokens, cotangent, routes, gate_probs, weight_in, weight_out, moment_in, square_in,
    moment_out, square_out, parents, own_rates, perturbed,
):
    members = lax.axis_size("member") // 2
    member = lax.axis_index("member") // 2
    expert = lax.axis_index("expert")
    ids = jnp.arange(members, dtype=jnp.int32)
    copies = parents != ids
    rate = jnp.sum(jnp.where(ids == member, jnp.where(copies, perturbed, own_rates), 0.0)).reshape(1)
    hid = weight_in.shape[1]
    named = jnp.stack([expert // 2 * 2 + expert % 2, expert // 2 * 2 + 1 - expert % 2,
                       (1 - expert // 2) * 2 + expert % 2, (1 - expert // 2) * 2 + 1 - expert % 2])
    table = jnp.sum(
        jnp.where(routes[None, :, :] == named[:, None, None], gate_probs.astype(jnp.float32)[None], 0.0), axis=2
    )
    gates = jnp.broadcast_to(table[:, :, None].astype(jnp.bfloat16), (4, tokens.shape[0], hid))
    link = ids[:, None]
    right_use = jnp.sum(copies[None] & (ids[None] > link) & (parents[None] <= link), axis=1)
    left_use = jnp.sum(copies[None] & (ids[None] <= link) & (parents[None] > link), axis=1)
    crowded = jnp.maximum(jnp.max(right_use), jnp.max(left_use)) > 1
    order = jnp.sum((copies[None, :] & (ids[None, :] < ids[:, None])).astype(jnp.int32), axis=1)

    def flags_for(rounds):
        rows = []
        for r in range(rounds):
            mine = copies & (order % rounds == r)
            rows.append(jnp.stack([
                jnp.any(mine & (parents == member) & (ids > member)),
                jnp.any(mine & (parents == member) & (ids < member)),
                jnp.any(mine & (ids == member) & (parents < member)),
                jnp.any(mine & (ids == member) & (parents > member)),
            ]))
        return jnp.stack(rows).astype(jnp.int32)

    rest = (rate, tokens, cotangent, gates, weight_in, weight_out, moment_in, square_in, moment_out, square_out)
    return lax.cond(
        crowded,
        lambda: tuple(fused_call(2, members, (flags_for(2), *rest))),
        lambda: tuple(fused_call(1, members, (flags_for(1), *rest))),
    )


def solution(mesh):
    fused = mesh.shape["member"] // 4 <= 2 and mesh.shape["expert"] == 4
    in_specs = (
        P(("member", "expert"), None),
        P(("member", "expert"), None),
        P(("member", "expert"), None),
        P(("member", "expert"), None),
        P("member", "expert"),
        P("member", "expert"),
        P("member", "expert"),
        P("member", "expert"),
        P("member", "expert"),
        P("member", "expert"),
        P(),
        P(),
        P(),
    )
    out_specs = (P("member", "expert"), P("member", "expert"), P(("member", "expert"), None))
    return jax.shard_map(
        on_device_fused if fused else on_device, mesh=mesh, in_specs=in_specs, out_specs=out_specs, check_vma=False
    )
```
